256 devices in a mesh: prow: 8 (over z), pcol: 8 (over y_hi, x), orb: 4 (over y_lo, core).
Axes of the slice: x: 4, y: 4 (y_hi: 2, y_lo: 2; y = y_hi * 2 + y_lo), z: 8, core: 2. Of those that a mesh axis runs over, the one named last changes fastest.
Arguments:
- panel_orbitals: bfloat16 [20000, 512], P('orb', ('prow', 'pcol')), may hold values from -8 to 8
- orbitals: bfloat16 [20000, 65536], P('orb', ('prow', 'pcol')), may hold values from -6 to 6
Outputs:
- coupling: float32 [512, 65536], P(None, ('prow', 'pcol', 'orb'))
The draws below stay inside these ranges and needn't reach their ends.
All inputs are finite; a program needn't handle non-finite values.
Results may differ from the reference program's by a relative error of at most 0.00035.
Values may be sent and summed in bfloat16 or wider, within the bound.
No kernel may reach another device: no remote copies, remote signals or barrier semaphores. Data moves between devices by JAX's collectives and lax.ppermute only.
A program may use at most 128 MiB of HBM per device.

```python
import jax
import jax.numpy as jnp
from jax import lax

NORB = 20000
PANEL = 512
PTS_DEV = 1024
NW = 65536


def draw_panel_orbitals(key, part):
    key = jax.random.fold_in(key, 7)
    source = jax.random.truncated_normal(key, -4.0, 4.0, (NORB, PANEL + 2), jnp.float32)
    mixed = source[:, 1:-1] + 0.5 * (source[:, :-2] + source[:, 2:])
    return mixed.astype(jnp.bfloat16)


def block_scale(stream_key, shape, cuts, low, largest):
    def one(dim, blocks):
        heights = jax.random.uniform(jax.random.fold_in(jax.random.fold_in(stream_key, 6), dim), (blocks,), jnp.float32, low / len(cuts), largest / len(cuts))
        return jnp.repeat(jnp.exp(heights), shape[dim] // blocks).reshape((-1,) + (1,) * (len(shape) - dim - 1))

    level = one(*cuts[0])
    for cut in cuts[1:]:
        level = level * one(*cut)
    return level


def bell_draw(stream_key, extent, deviation, reach, cuts=(), kind=jnp.bfloat16):
    drawn = jax.random.normal(stream_key, extent, jnp.float32) * deviation
    if len(cuts) > 0:
        drawn = block_scale(stream_key, extent, cuts, -0.22, 0.18) * drawn
    return jnp.clip(drawn, min=-reach, max=reach).astype(kind)


def setup_inputs(seed: int = 0) -> dict:
    streams_of = jax.random.split(jax.random.key(seed), 3)
    return {
        "panel_orbitals": draw_panel_orbitals(jax.random.fold_in(streams_of[2], 71), 0),
        "orbitals": bell_draw(streams_of[1], (NORB, NW), 1.0, 6.0, ((0, 4), (1, 64))),
    }


def reference(panel_orbitals, orbitals):
    contract = (((0,), (0,)), ((), ()))
    panel_gram = lax.dot_general(panel_orbitals.astype(jnp.float32), panel_orbitals.astype(jnp.float32), contract, preferred_element_type=jnp.float32)
    factor = jnp.linalg.cholesky(panel_gram * panel_gram)

    def one_block(position):
        column_block = lax.dynamic_slice_in_dim(orbitals, position * PTS_DEV, PTS_DEV, 1)
        gram_rows = lax.dot_general(panel_orbitals.astype(jnp.float32), column_block.astype(jnp.float32), contract, preferred_element_type=jnp.float32)
        return jax.scipy.linalg.solve_triangular(factor, gram_rows * gram_rows, lower=True)
    blocks = lax.map(one_block, jnp.arange(NW // PTS_DEV, dtype=jnp.int32))
    return jnp.transpose(blocks, (1, 0, 2)).reshape(PANEL, NW)
```

```python
import jax
import jax.numpy as jnp
from jax import lax
from jax.experimental import pallas as pl
from jax.experimental.pallas import tpu as pltpu
from jax.sharding import PartitionSpec as P

F32 = jnp.float32
HI = lax.Precision.HIGHEST
ROW0 = (((0,), (0,)), ((), ()))
NB = 128

CORE_SWAP = [(0, 1), (1, 0), (2, 3), (3, 2)]
CHIP_SWAP = [(0, 2), (2, 0), (1, 3), (3, 1)]


def x_shift(k):
    return [(h * 4 + x, h * 4 + (x + k) % 4) for h in range(2) for x in range(4)]


Y_SWAP = [(c, (c + 4) % 8) for c in range(8)]


def spread(v):
    return jnp.broadcast_to(v, (8, NB))


def reciprocal(v):
    r = pl.reciprocal(v, approx=True)
    r = r * (2.0 - v * r)
    return r * (2.0 - v * r)


def inverse_factor(rows):
    rows = list(rows)
    lane = lax.broadcasted_iota(jnp.int32, (8, NB), 1)
    sub = lax.broadcasted_iota(jnp.int32, (8, NB), 0)
    at = [sub == s for s in range(8)]
    groups, out = len(rows), []
    for q in range(groups):
        b = 8 * q
        w = rows[q]
        cols = [spread(w[:, b + t : b + t + 1]) for t in range(8)]
        a = {(s, t): spread(cols[t][s : s + 1, :]) for t in range(8) for s in range(t, 8)}
        here = (lane >= b) & (lane < b + 8)
        w = jnp.where(here, jnp.where(lane - b == sub, 1.0, 0.0), w)
        below = {}
        for g in range(q + 1, groups):
            for t in range(8):
                below[g, t] = spread(rows[g][:, b + t : b + t + 1])
            rows[g] = jnp.where(here, 0.0, rows[g])
        scale = jnp.zeros((8, NB), F32)
        for t in range(8):
            d = a[t, t]
            r = reciprocal(d)
            root = lax.rsqrt(d)
            root = root * (1.5 - (0.5 * d * root) * root)
            scale = jnp.where(at[t], root, scale)
            m = {s: a[s, t] * r for s in range(t + 1, 8)}
            for u in range(t + 1, 8):
                for s in range(u, 8):
                    a[s, u] = a[s, u] - m[s] * a[u, t]
            pivot_row = spread(w[t : t + 1, :])
            if t < 7:
                m_col = jnp.zeros((8, NB), F32)
                for s in range(t + 1, 8):
                    m_col = jnp.where(at[s], m[s], m_col)
                w = w - m_col * pivot_row
            for g in range(q + 1, groups):
                mg = below[g, t] * r
                for u in range(t + 1, 8):
                    below[g, u] = below[g, u] - mg * a[u, t]
                rows[g] = rows[g] - mg * pivot_row
        out.append(jnp.where(lane <= sub + b, w * scale, 0.0))
    return out


def factor_kernel(gram_ref, inv_ref, upper_ref, pair_ref):
    pair_ref[...] = gram_ref[...] * gram_ref[...]

    def step(j, carry):
        o = pl.multiple_of(j * NB, NB)
        rows = [pair_ref[pl.ds(o + 8 * q, 8), pl.ds(o, NB)] for q in range(NB // 8)]
        inv = jnp.concatenate(inverse_factor(rows), 0)
        inv_ref[j] = inv
        upper = jnp.dot(inv, pair_ref[pl.ds(o, NB), :], precision=HI, preferred_element_type=F32)
        upper_ref[j] = upper
        pair_ref[...] -= lax.dot_general(
            upper, upper, ROW0, precision=HI, preferred_element_type=F32
        )
        return carry

    lax.fori_loop(0, gram_ref.shape[0] // NB, step, 0)


def solve_kernel(inv_ref, upper_ref, mine_ref, other_ref, out_ref):
    blocks = inv_ref.shape[0]
    solved = []
    for j in range(blocks):
        cut = slice(j * NB, (j + 1) * NB)
        gram = mine_ref[cut, :] + other_ref[cut, :]
        rest = gram * gram
        for i in range(j):
            rest -= lax.dot_general(
                upper_ref[i, :, cut], solved[i], ROW0, precision=HI, preferred_element_type=F32
            )
        x = jnp.dot(inv_ref[j], rest, precision=HI, preferred_element_type=F32)
        solved.append(x)
        out_ref[cut, :] = x


def factorise(gram):
    n = gram.shape[0]
    blocks = n // NB
    return pl.pallas_call(
        factor_kernel,
        out_shape=(
            jax.ShapeDtypeStruct((blocks, NB, NB), F32),
            jax.ShapeDtypeStruct((blocks, NB, n), F32),
        ),
        scratch_shapes=[pltpu.VMEM((n, n), F32)],
        compiler_params=pltpu.CompilerParams(vmem_limit_bytes=40 << 20),
        cost_estimate=pl.CostEstimate(flops=30_000_000_000, bytes_accessed=3 << 20, transcendentals=0),
        name="factor",
    )(gram)


def solve(inv, upper, mine, other):
    return pl.pallas_call(
        solve_kernel,
        out_shape=jax.ShapeDtypeStruct(mine.shape, F32),
        compiler_params=pltpu.CompilerParams(vmem_limit_bytes=40 << 20),
        name="solve",
    )(inv, upper, mine, other)


def gather_panel(panel):
    own = panel.T
    y_hi = lax.axis_index("pcol") // 4
    x = lax.axis_index("pcol") % 4
    far = lax.ppermute(own, "pcol", Y_SWAP)
    first = y_hi == 0
    pair = jnp.stack([jnp.where(first, own, far), jnp.where(first, far, own)])
    turn = [pair] + [lax.ppermute(pair, "pcol", x_shift(k)) for k in (1, 2, 3)]
    ring = jnp.stack(turn[::-1] + turn[::-1])
    ring = lax.dynamic_slice_in_dim(ring, 3 - x, 4, 0)
    plane = ring.transpose(1, 0, 2, 3).reshape(64, -1)
    return lax.all_gather(plane, "prow", axis=0, tiled=True)


def on_device(panel_orbitals, orbitals):
    core = lax.axis_index("orb") % 2
    chip = lax.axis_index("orb") // 2
    full = gather_panel(panel_orbitals)
    panel = lax.dot_general(full, full, (((1,), (1,)), ((), ())), preferred_element_type=F32)
    half = panel.shape[0] // 2

    def rows_of(v, which):
        return lax.dynamic_slice_in_dim(v, which * half, half, 0)

    summed = rows_of(panel, core) + lax.ppermute(rows_of(panel, 1 - core), "orb", CORE_SWAP)
    summed = summed + lax.ppermute(summed, "orb", CHIP_SWAP)
    other = lax.ppermute(summed, "orb", CORE_SWAP)
    first = core == 0
    gram = jnp.concatenate([jnp.where(first, summed, other), jnp.where(first, other, summed)], 0)
    inv, upper = factorise(gram)

    rows = lax.dot_general(full, orbitals, (((1,), (0,)), ((), ())), preferred_element_type=F32)
    quarter = rows.shape[1] // 4

    def share(v, which):
        return lax.dynamic_slice_in_dim(v, which * quarter, quarter, 1)

    give = jnp.concatenate([share(rows, 1 - core), share(rows, 3 - core)], 1)
    keep = jnp.concatenate([share(rows, core), share(rows, 2 + core)], 1)
    on_chip = keep + lax.ppermute(give, "orb", CORE_SWAP)
    mine = share(on_chip, chip)
    arrived = lax.ppermute(share(on_chip, 1 - chip), "orb", CHIP_SWAP)
    return solve(inv, upper, mine, arrived)


def solution(mesh):
    return jax.shard_map(
        on_device,
        mesh=mesh,
        in_specs=(P("orb", ("prow", "pcol")), P("orb", ("prow", "pcol"))),
        out_specs=P(None, ("prow", "pcol", "orb")),
        check_vma=False,
    )
```

```python
import jax
import jax.numpy as jnp
from jax import lax
from jax.experimental import pallas as pl
from jax.experimental.pallas import tpu as pltpu
from jax.sharding import PartitionSpec as P

F32 = jnp.float32
HI = lax.Precision.HIGHEST
ROW0 = (((0,), (0,)), ((), ()))
NB = 128
PANEL = 512
HALF_K = 2560
CHUNK_K = 512
HALVES = (((0, 0), (0, 1), (0, 2), (0, 3), (3, 3)), ((1, 1), (1, 2), (1, 3), (2, 2), (2, 3)))

CORE_SWAP = [(0, 1), (1, 0), (2, 3), (3, 2)]
CHIP_SWAP = [(0, 2), (2, 0), (1, 3), (3, 1)]


def x_shift(k):
    return [(h * 4 + x, h * 4 + (x + k) % 4) for h in range(2) for x in range(4)]


Y_SWAP = [(c, (c + 4) % 8) for c in range(8)]


def spread(v):
    return jnp.broadcast_to(v, (8, NB))


def reciprocal(v):
    return pl.reciprocal(v, approx=True)


def held_group(q):
    z, rest = divmod(q, 8)
    y, x = divmod(rest, 4)
    return z * 8 + x * 2 + y


def three_way(v):
    high = v.astype(jnp.bfloat16).astype(F32)
    v = v - high
    mid = v.astype(jnp.bfloat16).astype(F32)
    return high, mid, v - mid


def inverse_factor(rows):
    rows = list(rows)
    groups, near_by, out = len(rows), 3, []
    lane = lax.broadcasted_iota(jnp.int32, (8, NB), 1)
    sub = lax.broadcasted_iota(jnp.int32, (8, NB), 0)
    at = [sub == s for s in range(8)]
    true_lane = (lane // 64) * 64 + ((lane // 8) % 2) * 32 + ((lane // 16) % 4) * 8 + lane % 8

    def lanes(v, b):
        return [spread(v[:, b + t : b + t + 1]) for t in range(8)]

    def row(v, s):
        return spread(v[s : s + 1, :])

    diag = lanes(rows[0], 8 * held_group(0))
    for q in range(groups):
        b = 8 * held_group(q)
        a = {(s, t): row(diag[t], s) for t in range(8) for s in range(t, 8)}
        here = (lane >= b) & (lane < b + 8)
        w = jnp.where(here, jnp.where(lane - b == sub, 1.0, 0.0), rows[q])
        near = range(q + 1, min(q + 1 + near_by, groups))
        far = range(q + 1 + near_by, groups)
        if q + 1 < groups:
            diag = lanes(rows[q + 1], 8 * held_group(q + 1))
        below = {g: lanes(rows[g], b) for g in near}
        for g in range(q + 1, groups):
            rows[g] = jnp.where(here, 0.0, rows[g])
        pivots = jnp.ones((8, NB), F32)
        for t in range(8):
            d = a[t, t]
            if t < 7:
                square = a[t + 1, t] * a[t + 1, t]
            r = reciprocal(d)
            pivots = jnp.where(at[t], d, pivots)
            m = {s: a[s, t] * r for s in range(t + 1, 8)}
            for u in range(t + 1, 8):
                for s in range(u, 8):
                    step = square * r if s == t + 1 else m[s] * a[u, t]
                    a[s, u] = a[s, u] - step
            if q + 1 < groups:
                mg = below[q + 1][t] * r
                for u in range(8):
                    diag[u] = diag[u] - mg * row(below[q + 1][t], u)
            pivot_row = row(w, t)
            if t < 7:
                m_col = jnp.zeros((8, NB), F32)
                for s in range(t + 1, 8):
                    m_col = jnp.where(at[s], m[s], m_col)
                w = w - m_col * pivot_row
            for g in near:
                mg = below[g][t] * r
                for u in range(t + 1, 8):
                    below[g][u] = below[g][u] - mg * a[u, t]
                rows[g] = rows[g] - mg * pivot_row
        if len(far):
            ah, am, al = three_way(w * reciprocal(pivots))
            bh, bm, bl = three_way(w)
            product = lax.dot_general(
                jnp.concatenate([ah, ah, am, ah, am, al], 0).astype(jnp.bfloat16),
                jnp.concatenate([bh, bm, bh, bl, bm, bh], 0).astype(jnp.bfloat16),
                ROW0,
                preferred_element_type=F32,
            )
            for g in far:
                h = 8 * held_group(g)
                rows[g] = rows[g] - product[h : h + 8]
        root = lax.rsqrt(pivots)
        root = root * (1.5 - (0.5 * pivots * root) * root)
        out.append(jnp.where(true_lane <= sub + 8 * q, w * root, 0.0))
    return out


def factor_kernel(mine_ref, other_ref, inv_ref, upper_ref, pair_ref):
    core = lax.axis_index("orb") % 2

    def place(ref, half):
        for k, (i, j) in enumerate(HALVES[half]):
            gram = ref[k]
            pair_ref[i * NB : (i + 1) * NB, j * NB : (j + 1) * NB] = gram * gram

    @pl.when(core == 0)
    def _():
        place(mine_ref, 0)
        place(other_ref, 1)

    @pl.when(core == 1)
    def _():
        place(other_ref, 0)
        place(mine_ref, 1)

    def step(j, carry):
        o = pl.multiple_of(j * NB, NB)
        rows = [
            pair_ref[pl.ds(o + 8 * held_group(q), 8), pl.ds(o, NB)] for q in range(NB // 8)
        ]
        inv = jnp.concatenate(inverse_factor(rows), 0)
        inv_ref[j] = inv
        for k in range(PANEL // NB - 1):

            @pl.when(j == k)
            def _():
                rest = (k + 1) * NB
                upper = jnp.dot(
                    inv,
                    pair_ref[k * NB : rest, rest:],
                    precision=HI,
                    preferred_element_type=F32,
                )
                upper_ref[k, :, rest:] = upper
                for i in range(rest, PANEL, NB):
                    pair_ref[i : i + NB, i:] -= lax.dot_general(
                        upper[:, i - rest : i - rest + NB],
                        upper[:, i - rest :],
                        ROW0,
                        precision=HI,
                        preferred_element_type=F32,
                    )

        return carry

    lax.fori_loop(0, PANEL // NB, step, 0)


def solve_kernel(inv_ref, upper_ref, keep_ref, arrived_ref, other_ref, out_ref, gram_ref, sems):
    chip = lax.axis_index("orb") // 2
    copies = [
        pltpu.make_async_copy(ref.at[chip], gram_ref.at[k], sems.at[k])
        for k, ref in enumerate((keep_ref, arrived_ref))
    ]
    for copy in copies:
        copy.start()
    for copy in copies:
        copy.wait()
    solved = []
    for j in range(PANEL // NB):
        cut = slice(j * NB, (j + 1) * NB)
        gram = gram_ref[0, cut, :] + gram_ref[1, cut, :] + other_ref[cut, :]
        rest = gram * gram
        for i in range(j):
            rest -= lax.dot_general(
                upper_ref[i, :, cut], solved[i], ROW0, precision=HI, preferred_element_type=F32
            )
        x = jnp.dot(inv_ref[j], rest, precision=HI, preferred_element_type=F32)
        solved.append(x)
        out_ref[cut, :] = x


def factorise(mine, other):
    blocks = PANEL // NB
    return pl.pallas_call(
        factor_kernel,
        out_shape=(
            jax.ShapeDtypeStruct((blocks, NB, NB), F32),
            jax.ShapeDtypeStruct((blocks - 1, NB, PANEL), F32),
        ),
        scratch_shapes=[pltpu.VMEM((PANEL, PANEL), F32)],
        compiler_params=pltpu.CompilerParams(vmem_limit_bytes=40 << 20),
        cost_estimate=pl.CostEstimate(flops=30_000_000_000, bytes_accessed=3 << 20, transcendentals=0),
        name="factor",
    )(mine, other)


def solve(inv, upper, keep, arrived, other):
    vmem, hbm = pl.BlockSpec(memory_space=pltpu.VMEM), pl.BlockSpec(memory_space=pl.ANY)
    return pl.pallas_call(
        solve_kernel,
        in_specs=[vmem, vmem, hbm, hbm, vmem],
        out_shape=jax.ShapeDtypeStruct(other.shape, F32),
        scratch_shapes=[pltpu.VMEM((2,) + other.shape, F32), pltpu.SemaphoreType.DMA((2,))],
        compiler_params=pltpu.CompilerParams(vmem_limit_bytes=40 << 20),
        name="solve",
    )(inv, upper, keep, arrived, other)


def z_shift(k):
    return [(z, (z + k) % 8) for z in range(8)]


def along_z(k, v):
    return lax.ppermute(v, "prow", z_shift(k))


def along_x(k, v):
    return lax.ppermute(v, "pcol", x_shift(k))


def gather_panel(panel):
    own = jnp.pad(panel.T, ((0, 0), (0, 2 * HALF_K - panel.shape[0])))
    far = lax.ppermute(own, "pcol", Y_SWAP)
    first = lax.axis_index("pcol") < 4
    pair = jnp.where(first, jnp.concatenate([own, far], 0), jnp.concatenate([far, own], 0))
    left, right = pair[:, :HALF_K], pair[:, HALF_K:]

    x_steps = (0, -1, 1, 2)
    plane = jnp.concatenate([left, along_x(1, left), along_x(-1, left), along_x(2, left)], 0)
    pieces, places = [plane], [(0, 16 * k, 0, 0, s) for k, s in enumerate(x_steps)]
    up = down = plane
    for s in range(1, 5):
        up = along_z(1, up)
        places += [(len(pieces), 16 * k, 0, -s, t) for k, t in enumerate(x_steps)]
        pieces.append(up)
        if s < 4:
            down = along_z(-1, down)
            places += [(len(pieces), 16 * k, 0, s, t) for k, t in enumerate(x_steps)]
            pieces.append(down)

    z_steps, column = [0], [right]
    up = down = right
    for s in range(1, 5):
        up = along_z(1, up)
        z_steps.append(-s)
        column.append(up)
        if s < 4:
            down = along_z(-1, down)
            z_steps.append(s)
            column.append(down)
    column = jnp.concatenate(column, 0)
    half = column.shape[0] // 2
    up, down = along_x(1, column), along_x(-1, column)
    for piece, t, r in (
        (column, 0, range(8)),
        (up, -1, range(8)),
        (down, 1, range(8)),
        (along_x(1, up[:half]), 2, range(4)),
        (along_x(-1, down[half:]), 2, range(4, 8)),
    ):
        places += [(len(pieces), 16 * k, 1, z_steps[m], t) for k, m in enumerate(r)]
        pieces.append(piece)
    return pieces, places


def load_panel(places, piece_refs, panel_ref, sems):
    z = lax.axis_index("prow")
    x = lax.axis_index("pcol") % 4
    for piece, row, half, dz, dx in places:
        to = lax.rem(z + dz + 8, 8) * 64 + lax.rem(x + dx + 4, 4) * 16
        pltpu.make_async_copy(
            piece_refs[piece].at[pl.ds(row, 16), :],
            panel_ref.at[half, pl.ds(pl.multiple_of(to, 16), 16), :],
            sems.at[half],
        ).start()


def wait_panel(panel_ref, sems, half):
    pltpu.make_async_copy(panel_ref.at[half], panel_ref.at[half], sems.at[half]).wait()


def panel_gram_kernel(places, pieces, *refs):
    piece_refs, (out_ref, panel_ref, sems) = refs[:pieces], refs[pieces:]
    load_panel(places, piece_refs, panel_ref, sems)
    strips = [None, None]
    for half in range(2):
        wait_panel(panel_ref, sems, half)
        for s in range(2):
            part = lax.dot_general(
                panel_ref[half, s * 256 : (s + 1) * 256, :],
                panel_ref[half, s * 256 :, :],
                (((1,), (1,)), ((), ())),
                preferred_element_type=F32,
            )
            strips[s] = part if half == 0 else strips[s] + part
    for h, blocks in enumerate(HALVES):
        for k, (i, j) in enumerate(blocks):
            s = i // 2
            out_ref[h, k] = strips[s][
                (i - 2 * s) * NB : (i - 2 * s + 1) * NB, (j - 2 * s) * NB : (j - 2 * s + 1) * NB
            ]


def panel_gram(pieces, places):
    return pl.pallas_call(
        lambda *refs: panel_gram_kernel(places, len(pieces), *refs),
        in_specs=[pl.BlockSpec(memory_space=pl.ANY)] * len(pieces),
        out_shape=jax.ShapeDtypeStruct((2, 5, NB, NB), F32),
        scratch_shapes=[pltpu.VMEM((2, PANEL, HALF_K), jnp.bfloat16), pltpu.SemaphoreType.DMA((2,))],
        compiler_params=pltpu.CompilerParams(vmem_limit_bytes=60 << 20),
        cost_estimate=pl.CostEstimate(flops=3_000_000_000, bytes_accessed=8 << 20, transcendentals=0),
        name="panel_gram",
    )(*pieces)


def row_gram_kernel(places, pieces, *refs):
    piece_refs = refs[:pieces]
    orbitals_ref, give_ref, keep_ref, panel_ref, window_ref, total_ref, sems, window_sems = refs[pieces:]
    core = lax.axis_index("orb") % 2
    load_panel(places, piece_refs, panel_ref, sems)
    rows = orbitals_ref.shape[0]
    window_ref[rows:, :] = jnp.zeros((2 * HALF_K - rows, orbitals_ref.shape[1]), jnp.bfloat16)
    copies = []
    for k in range(0, rows, CHUNK_K):
        part = pl.ds(k, min(CHUNK_K, rows - k))
        copies.append(
            pltpu.make_async_copy(
                orbitals_ref.at[part, :], window_ref.at[part, :], window_sems.at[len(copies)]
            )
        )
        copies[-1].start()
    for k, copy in enumerate(copies):
        half, at = divmod(k * CHUNK_K, HALF_K)
        if at == 0:
            wait_panel(panel_ref, sems, half)
        copy.wait()
        part = jnp.dot(
            panel_ref[half, :, at : at + CHUNK_K],
            window_ref[k * CHUNK_K : (k + 1) * CHUNK_K, :],
            preferred_element_type=F32,
        )
        quarter = part.shape[1] // 4
        for n in range(4):
            value = part[:, n * quarter : (n + 1) * quarter]
            total_ref[n] = value if k == 0 else total_ref[n] + value
    sends = []
    for c in range(2):
        for ref, which in ((give_ref, 1 - core), (keep_ref, core)):
            sends.append(
                pltpu.make_async_copy(total_ref.at[2 * c + which], ref.at[c], window_sems.at[len(sends)])
            )
            sends[-1].start()
    for send in sends:
        send.wait()


def row_gram(pieces, places, orbitals):
    rows, columns = orbitals.shape
    out = jax.ShapeDtypeStruct((2, PANEL, columns // 4), F32)
    return pl.pallas_call(
        lambda *refs: row_gram_kernel(places, len(pieces), *refs),
        in_specs=[pl.BlockSpec(memory_space=pl.ANY)] * (len(pieces) + 1),
        out_specs=[pl.BlockSpec(memory_space=pl.ANY)] * 2,
        out_shape=(out, out),
        scratch_shapes=[
            pltpu.VMEM((2, PANEL, HALF_K), jnp.bfloat16),
            pltpu.VMEM((2 * HALF_K, columns), jnp.bfloat16),
            pltpu.VMEM((4, PANEL, columns // 4), F32),
            pltpu.SemaphoreType.DMA((2,)),
            pltpu.SemaphoreType.DMA((2 * HALF_K // CHUNK_K,)),
        ],
        compiler_params=pltpu.CompilerParams(vmem_limit_bytes=60 << 20),
        cost_estimate=pl.CostEstimate(flops=6_000_000_000, bytes_accessed=17 << 20, transcendentals=0),
        name="row_gram",
    )(*pieces, orbitals)


def swap_cores(v):
    return lax.ppermute(v, "orb", CORE_SWAP)


def swap_chips(v):
    return lax.ppermute(v, "orb", CHIP_SWAP)


def pick(v, which):
    return lax.dynamic_index_in_dim(v, which, 0, keepdims=False)


def on_device(panel_orbitals, orbitals):
    core = lax.axis_index("orb") % 2
    chip = lax.axis_index("orb") // 2
    pieces, places = gather_panel(panel_orbitals)

    panel = panel_gram(pieces, places)
    half = pick(panel, core) + swap_cores(pick(panel, 1 - core))
    half, pieces = lax.optimization_barrier((half, pieces))
    half = half + swap_chips(half)
    give, keep = row_gram(pieces, places, orbitals)
    half, give = lax.optimization_barrier((half, give))
    arrived = swap_cores(give)
    other = swap_chips(pick(keep, 1 - chip) + pick(arrived, 1 - chip))
    inv, upper = factorise(half, swap_cores(half))
    return solve(inv, upper, keep, arrived, other)


def solution(mesh):
    return jax.shard_map(
        on_device,
        mesh=mesh,
        in_specs=(P("orb", ("prow", "pcol")), P("orb", ("prow", "pcol"))),
        out_specs=P(None, ("prow", "pcol", "orb")),
        check_vma=False,
    )
```

```python
import jax
import jax.numpy as jnp
from jax import lax
from jax.experimental import pallas as pl
from jax.experimental.pallas import tpu as pltpu
from jax.sharding import PartitionSpec as P

F32 = jnp.float32
HI = lax.Precision.HIGHEST
ROW0 = (((0,), (0,)), ((), ()))
NB = 128
PANEL = 512
FIRST_K = 2432
SECOND_K = 2688
CHUNK_K = 1024
HALVES = (((0, 0), (0, 1), (0, 2), (0, 3), (3, 3)), ((1, 1), (1, 2), (1, 3), (2, 2), (2, 3)))

CORE_SWAP = [(0, 1), (1, 0), (2, 3), (3, 2)]
CHIP_SWAP = [(0, 2), (2, 0), (1, 3), (3, 1)]


def x_shift(k):
    return [(h * 4 + x, h * 4 + (x + k) % 4) for h in range(2) for x in range(4)]


Y_SWAP = [(c, (c + 4) % 8) for c in range(8)]


def spread(v):
    return jnp.broadcast_to(v, (8, NB))


def reciprocal(v):
    return pl.reciprocal(v, approx=True)


def held_group(q):
    z, rest = divmod(q, 8)
    y, x = divmod(rest, 4)
    return z * 8 + x * 2 + y


def three_way(v):
    high = v.astype(jnp.bfloat16).astype(F32)
    v = v - high
    mid = v.astype(jnp.bfloat16).astype(F32)
    return high, mid, v - mid


def inverse_factor(rows):
    rows = list(rows)
    groups, near_by, out = len(rows), 3, []
    lane = lax.broadcasted_iota(jnp.int32, (8, NB), 1)
    sub = lax.broadcasted_iota(jnp.int32, (8, NB), 0)
    at = [sub == s for s in range(8)]
    true_lane = (lane // 64) * 64 + ((lane // 8) % 2) * 32 + ((lane // 16) % 4) * 8 + lane % 8

    def lanes(v, b):
        return [spread(v[:, b + t : b + t + 1]) for t in range(8)]

    def row(v, s):
        return spread(v[s : s + 1, :])

    diag = lanes(rows[0], 8 * held_group(0))
    for q in range(groups):
        b = 8 * held_group(q)
        a = {(s, t): row(diag[t], s) for t in range(8) for s in range(t, 8)}
        here = (lane >= b) & (lane < b + 8)
        w = jnp.where(here, jnp.where(lane - b == sub, 1.0, 0.0), rows[q])
        near = range(q + 1, min(q + 1 + near_by, groups))
        far = range(q + 1 + near_by, groups)
        if q + 1 < groups:
            diag = lanes(rows[q + 1], 8 * held_group(q + 1))
        below = {g: lanes(rows[g], b) for g in near}
        for g in range(q + 1, groups):
            rows[g] = jnp.where(here, 0.0, rows[g])
        pivots = jnp.ones((8, NB), F32)
        for t in range(8):
            d = a[t, t]
            if t < 7:
                square = a[t + 1, t] * a[t + 1, t]
            r = reciprocal(d)
            pivots = jnp.where(at[t], d, pivots)
            m = {s: a[s, t] * r for s in range(t + 1, 8)}
            for u in range(t + 1, 8):
                for s in range(u, 8):
                    step = square * r if s == t + 1 else m[s] * a[u, t]
                    a[s, u] = a[s, u] - step
            if q + 1 < groups:
                mg = below[q + 1][t] * r
                for u in range(8):
                    diag[u] = diag[u] - mg * row(below[q + 1][t], u)
            pivot_row = row(w, t)
            if t < 7:
                m_col = jnp.zeros((8, NB), F32)
                for s in range(t + 1, 8):
                    m_col = jnp.where(at[s], m[s], m_col)
                w = w - m_col * pivot_row
            for g in near:
                mg = below[g][t] * r
                for u in range(t + 1, 8):
                    below[g][u] = below[g][u] - mg * a[u, t]
                rows[g] = rows[g] - mg * pivot_row
        if len(far):
            ah, am, al = three_way(w * reciprocal(pivots))
            bh, bm, bl = three_way(w)
            product = lax.dot_general(
                jnp.concatenate([ah, ah, am, ah, am, al], 0).astype(jnp.bfloat16),
                jnp.concatenate([bh, bm, bh, bl, bm, bh], 0).astype(jnp.bfloat16),
                ROW0,
                preferred_element_type=F32,
            )
            for g in far:
                h = 8 * held_group(g)
                rows[g] = rows[g] - product[h : h + 8]
        root = lax.rsqrt(pivots)
        root = root * (1.5 - (0.5 * pivots * root) * root)
        out.append(jnp.where(true_lane <= sub + 8 * q, w * root, 0.0))
    return out


def factor_kernel(mine_ref, other_ref, inv_ref, upper_ref, pair_ref):
    core = lax.axis_index("orb") % 2

    def place(ref, half):
        for k, (i, j) in enumerate(HALVES[half]):
            gram = ref[k]
            pair_ref[i * NB : (i + 1) * NB, j * NB : (j + 1) * NB] = gram * gram

    @pl.when(core == 0)
    def _():
        place(mine_ref, 0)
        place(other_ref, 1)

    @pl.when(core == 1)
    def _():
        place(other_ref, 0)
        place(mine_ref, 1)

    def step(j, carry):
        o = pl.multiple_of(j * NB, NB)
        rows = [
            pair_ref[pl.ds(o + 8 * held_group(q), 8), pl.ds(o, NB)] for q in range(NB // 8)
        ]
        inv = jnp.concatenate(inverse_factor(rows), 0)
        inv_ref[j] = inv
        for k in range(PANEL // NB - 1):

            @pl.when(j == k)
            def _():
                rest = (k + 1) * NB
                upper = jnp.dot(
                    inv,
                    pair_ref[k * NB : rest, rest:],
                    precision=HI,
                    preferred_element_type=F32,
                )
                upper_ref[k, :, rest:] = upper
                for i in range(rest, PANEL, NB):
                    pair_ref[i : i + NB, i:] -= lax.dot_general(
                        upper[:, i - rest : i - rest + NB],
                        upper[:, i - rest :],
                        ROW0,
                        precision=HI,
                        preferred_element_type=F32,
                    )

        return carry

    lax.fori_loop(0, PANEL // NB, step, 0)


def solve_kernel(inv_ref, upper_ref, keep_ref, arrived_ref, other_ref, out_ref, gram_ref, sems):
    chip = lax.axis_index("orb") // 2
    copies = [
        pltpu.make_async_copy(ref.at[chip], gram_ref.at[k], sems.at[k])
        for k, ref in enumerate((keep_ref, arrived_ref))
    ]
    for copy in copies:
        copy.start()
    for copy in copies:
        copy.wait()
    solved = []
    for j in range(PANEL // NB):
        cut = slice(j * NB, (j + 1) * NB)
        gram = gram_ref[0, cut, :] + gram_ref[1, cut, :] + other_ref[cut, :]
        rest = gram * gram
        for i in range(j):
            rest -= lax.dot_general(
                upper_ref[i, :, cut], solved[i], ROW0, precision=HI, preferred_element_type=F32
            )
        x = jnp.dot(inv_ref[j], rest, precision=HI, preferred_element_type=F32)
        solved.append(x)
        out_ref[cut, :] = x


def factorise(mine, other):
    blocks = PANEL // NB
    return pl.pallas_call(
        factor_kernel,
        out_shape=(
            jax.ShapeDtypeStruct((blocks, NB, NB), F32),
            jax.ShapeDtypeStruct((blocks - 1, NB, PANEL), F32),
        ),
        scratch_shapes=[pltpu.VMEM((PANEL, PANEL), F32)],
        compiler_params=pltpu.CompilerParams(vmem_limit_bytes=40 << 20),
        cost_estimate=pl.CostEstimate(flops=30_000_000_000, bytes_accessed=3 << 20, transcendentals=0),
        name="factor",
    )(mine, other)


def solve(inv, upper, keep, arrived, other):
    vmem, hbm = pl.BlockSpec(memory_space=pltpu.VMEM), pl.BlockSpec(memory_space=pl.ANY)
    return pl.pallas_call(
        solve_kernel,
        in_specs=[vmem, vmem, hbm, hbm, vmem],
        out_shape=jax.ShapeDtypeStruct(other.shape, F32),
        scratch_shapes=[pltpu.VMEM((2,) + other.shape, F32), pltpu.SemaphoreType.DMA((2,))],
        compiler_params=pltpu.CompilerParams(vmem_limit_bytes=40 << 20),
        name="solve",
    )(inv, upper, keep, arrived, other)


def z_shift(k):
    return [(z, (z + k) % 8) for z in range(8)]


def along_z(k, v):
    return lax.ppermute(v, "prow", z_shift(k))


def along_x(k, v):
    return lax.ppermute(v, "pcol", x_shift(k))


def after(v, *others):
    return lax.optimization_barrier((v,) + others)[0]


def gather_panel(panel):
    own = panel.T
    far = lax.ppermute(own, "pcol", Y_SWAP)
    first = lax.axis_index("pcol") < 4
    pair = jnp.where(first, jnp.concatenate([own, far], 0), jnp.concatenate([far, own], 0))
    left = pair[:, :FIRST_K]
    right = jnp.pad(pair[:, FIRST_K:], ((0, 0), (0, FIRST_K + SECOND_K - panel.shape[0])))

    x_steps = (0, -1, 1, 2)
    plane = jnp.concatenate([left, along_x(1, left), along_x(-1, left), along_x(2, left)], 0)
    planes, plane_z = [plane], [0]
    column, column_z = [right], [0]

    def turn(pieces, steps, s, *ties):
        up, down = pieces[-2:] if s > 1 else pieces * 2
        pieces += [along_z(1, after(up, *ties)), along_z(-1, after(down, *ties))]
        steps += [-s, s]

    turn(column, column_z, 1)
    turn(planes, plane_z, 1)
    turn(column, column_z, 2)
    turn(column, column_z, 3, *planes[1:3])
    column_z.append(4)
    column.append(along_z(1, column[-2]))
    turn(planes, plane_z, 2)
    column = jnp.concatenate(column, 0)
    half = column.shape[0] // 2
    column = after(column, *planes[3:5])
    x_up, x_down = along_x(1, column), along_x(-1, column)
    turn(planes, plane_z, 3)
    x_far = (
        along_x(1, after(x_up[:half], *planes[5:7])),
        along_x(-1, after(x_down[half:], *planes[5:7])),
    )
    planes.append(along_z(1, planes[-2]))
    plane_z.append(4)

    plane_places = [
        (n, 16 * k, dz, dx) for n, dz in enumerate(plane_z) for k, dx in enumerate(x_steps)
    ]
    columns, column_places = [], []
    for piece, dx, units in (
        (column, 0, range(8)),
        (x_up, -1, range(8)),
        (x_down, 1, range(8)),
        (x_far[0], 2, range(4)),
        (x_far[1], 2, range(4, 8)),
    ):
        column_places += [(len(columns), 16 * k, column_z[m], dx) for k, m in enumerate(units)]
        columns.append(piece)
    return (planes, plane_places), (columns, column_places)


def chunks(depth):
    return [slice(k, min(k + CHUNK_K, depth)) for k in range(0, depth, CHUNK_K)]


def stream(places, piece_refs, panel_ref, sems, window=None):
    z = lax.axis_index("prow")
    x = lax.axis_index("pcol") % 4
    units = [
        (piece, row, pl.multiple_of(lax.rem(z + dz + 8, 8) * 64 + lax.rem(x + dx + 4, 4) * 16, 16))
        for piece, row, dz, dx in places
    ]
    parts = chunks(panel_ref.shape[1])

    def window_copy(c):
        orbitals_ref, start, window_ref, window_sems = window
        first = parts[c].start
        size = min(parts[c].stop, orbitals_ref.shape[0] - start) - first
        return pltpu.make_async_copy(
            orbitals_ref.at[pl.ds(start + first, size), :],
            window_ref.at[pl.ds(first, size), :],
            window_sems.at[c],
        )

    def start_chunk(c):
        for piece, row, to in units:
            pltpu.make_async_copy(
                piece_refs[piece].at[pl.ds(row, 16), parts[c]],
                panel_ref.at[pl.ds(to, 16), parts[c]],
                sems.at[c],
            ).start()
        if window is not None:
            window_copy(c).start()

    for c in range(min(2, len(parts))):
        start_chunk(c)
    for c, part in enumerate(parts):
        here = panel_ref.at[:, part]
        pltpu.make_async_copy(here, here, sems.at[c]).wait()
        if window is not None:
            window_copy(c).wait()
        if c + 2 < len(parts):
            start_chunk(c + 2)
        yield c, part


def add_rows(panel_ref, window_ref, part, total_ref, started):
    quarter = total_ref.shape[2]
    gram = jnp.dot(panel_ref[:, part], window_ref[part, :], preferred_element_type=F32)
    for n in range(4):
        value = gram[:, n * quarter : (n + 1) * quarter]
        total_ref[n] = total_ref[n] + value if started else value


def panel_strips(panel_ref, part, before):
    strips = []
    for s in range(2):
        strip = lax.dot_general(
            panel_ref[s * 256 : (s + 1) * 256, part],
            panel_ref[s * 256 :, part],
            (((1,), (1,)), ((), ())),
            preferred_element_type=F32,
        )
        strips.append(strip if before is None else before[s] + strip)
    return strips


def put_blocks(strips, out_ref, before_ref=None):
    for h, blocks in enumerate(HALVES):
        for k, (i, j) in enumerate(blocks):
            s = i // 2
            i, j = i - 2 * s, j - 2 * s
            value = strips[s][i * NB : (i + 1) * NB, j * NB : (j + 1) * NB]
            out_ref[h, k] = value if before_ref is None else before_ref[h, k] + value


def first_kernel(places, pieces, *refs):
    orbitals_ref, panel_out, rows_out = refs[pieces : pieces + 3]
    panel_ref, window_ref, total_ref, block_ref, sems, window_sems, out_sems = refs[pieces + 3 :]
    window = (orbitals_ref, 0, window_ref, window_sems)
    strips = None
    for c, part in stream(places, refs[:pieces], panel_ref, sems, window):
        add_rows(panel_ref, window_ref, part, total_ref, c > 0)
        if part.stop == FIRST_K:
            send_rows = pltpu.make_async_copy(total_ref, rows_out, out_sems.at[0])
            send_rows.start()
        strips = panel_strips(panel_ref, part, strips)
    put_blocks(strips, block_ref)
    send_panel = pltpu.make_async_copy(block_ref, panel_out, out_sems.at[1])
    send_panel.start()
    send_rows.wait()
    send_panel.wait()


def panel_kernel(places, pieces, *refs):
    before_ref, give_ref, keep_ref = refs[pieces : pieces + 3]
    panel_ref, total_ref, start_ref, sems, out_sems = refs[pieces + 3 :]
    core = lax.axis_index("orb") % 2
    strips = None
    for c, part in stream(places, refs[:pieces], panel_ref, sems):
        if c == 0:
            before = pltpu.make_async_copy(before_ref, start_ref, out_sems.at[2])
            before.start()
        strips = panel_strips(panel_ref, part, strips)
    before.wait()
    put_blocks(strips, total_ref, start_ref)
    sends = [
        pltpu.make_async_copy(total_ref.at[1 - core], give_ref, out_sems.at[0]),
        pltpu.make_async_copy(total_ref.at[core], keep_ref, out_sems.at[1]),
    ]
    for send in sends:
        send.start()
    for send in sends:
        send.wait()


def rows_kernel(places, pieces, *refs):
    orbitals_ref, before_ref, give_ref, keep_ref = refs[pieces : pieces + 4]
    panel_ref, window_ref, total_ref, start_ref, sems, window_sems, out_sems = refs[pieces + 4 :]
    core = lax.axis_index("orb") % 2
    quarter = total_ref.shape[2]
    rows = orbitals_ref.shape[0] - FIRST_K
    window_ref[rows:, :] = jnp.zeros((SECOND_K - rows, orbitals_ref.shape[1]), jnp.bfloat16)
    window = (orbitals_ref, FIRST_K, window_ref, window_sems)
    for c, part in stream(places, refs[:pieces], panel_ref, sems, window):
        if c == 0:
            before = pltpu.make_async_copy(before_ref, start_ref, out_sems.at[4])
            before.start()
        if part.stop < SECOND_K:
            add_rows(panel_ref, window_ref, part, total_ref, c > 0)
    before.wait()
    for n in range(4):
        gram = jnp.dot(
            panel_ref[:, part],
            window_ref[part, n * quarter : (n + 1) * quarter],
            preferred_element_type=F32,
        )
        total_ref[n] = total_ref[n] + (start_ref[n] + gram)
        if n % 2:
            sends = sends if n > 1 else []
            for ref, which in ((give_ref, 1 - core), (keep_ref, core)):
                sends.append(
                    pltpu.make_async_copy(
                        total_ref.at[n - 1 + which], ref.at[n // 2], out_sems.at[len(sends)]
                    )
                )
                sends[-1].start()
    for send in sends:
        send.wait()


HBM = pl.BlockSpec(memory_space=pl.ANY)
DMA = pltpu.SemaphoreType.DMA
ROOMY = pltpu.CompilerParams(vmem_limit_bytes=60 << 20)


def first_grams(pieces, places, orbitals):
    columns, count = orbitals.shape[1], len(chunks(FIRST_K))
    blocks, totals = (2, 5, NB, NB), (4, PANEL, columns // 4)
    return pl.pallas_call(
        lambda *refs: first_kernel(places, len(pieces), *refs),
        in_specs=[HBM] * (len(pieces) + 1),
        out_specs=[HBM] * 2,
        out_shape=(jax.ShapeDtypeStruct(blocks, F32), jax.ShapeDtypeStruct(totals, F32)),
        scratch_shapes=[
            pltpu.VMEM((PANEL, FIRST_K), jnp.bfloat16),
            pltpu.VMEM((FIRST_K, columns), jnp.bfloat16),
            pltpu.VMEM(totals, F32),
            pltpu.VMEM(blocks, F32),
            DMA((count,)),
            DMA((count,)),
            DMA((2,)),
        ],
        compiler_params=ROOMY,
        cost_estimate=pl.CostEstimate(flops=5_000_000_000, bytes_accessed=12 << 20, transcendentals=0),
        name="first_grams",
    )(*pieces, orbitals)


def panel_gram(pieces, places, before):
    out = jax.ShapeDtypeStruct((5, NB, NB), F32)
    return pl.pallas_call(
        lambda *refs: panel_kernel(places, len(pieces), *refs),
        in_specs=[HBM] * (len(pieces) + 1),
        out_specs=[HBM] * 2,
        out_shape=(out, out),
        scratch_shapes=[
            pltpu.VMEM((PANEL, SECOND_K), jnp.bfloat16),
            pltpu.VMEM((2, 5, NB, NB), F32),
            pltpu.VMEM((2, 5, NB, NB), F32),
            DMA((len(chunks(SECOND_K)),)),
            DMA((3,)),
        ],
        compiler_params=ROOMY,
        cost_estimate=pl.CostEstimate(flops=1_500_000_000, bytes_accessed=4 << 20, transcendentals=0),
        name="panel_gram",
    )(*pieces, before)


def row_gram(pieces, places, orbitals, before):
    columns, count = orbitals.shape[1], len(chunks(SECOND_K))
    out = jax.ShapeDtypeStruct((2, PANEL, columns // 4), F32)
    return pl.pallas_call(
        lambda *refs: rows_kernel(places, len(pieces), *refs),
        in_specs=[HBM] * (len(pieces) + 2),
        out_specs=[HBM] * 2,
        out_shape=(out, out),
        scratch_shapes=[
            pltpu.VMEM((PANEL, SECOND_K), jnp.bfloat16),
            pltpu.VMEM((SECOND_K, columns), jnp.bfloat16),
            pltpu.VMEM((4, PANEL, columns // 4), F32),
            pltpu.VMEM((4, PANEL, columns // 4), F32),
            DMA((count,)),
            DMA((count,)),
            DMA((5,)),
        ],
        compiler_params=ROOMY,
        cost_estimate=pl.CostEstimate(flops=4_000_000_000, bytes_accessed=12 << 20, transcendentals=0),
        name="row_gram",
    )(*pieces, orbitals, before)


def swap_cores(v):
    return lax.ppermute(v, "orb", CORE_SWAP)


def swap_chips(v):
    return lax.ppermute(v, "orb", CHIP_SWAP)


def pick(v, which):
    return lax.dynamic_index_in_dim(v, which, 0, keepdims=False)


def on_device(panel_orbitals, orbitals):
    chip = lax.axis_index("orb") // 2
    (first, first_places), (second, second_places) = gather_panel(panel_orbitals)
    panel, rows = first_grams(first, first_places, orbitals)
    give, keep = panel_gram(second, second_places, panel)
    half = keep + swap_cores(give)
    half, second = lax.optimization_barrier((half, second))
    half = half + swap_chips(half)
    give, keep = row_gram(second, second_places, orbitals, rows)
    half, give = lax.optimization_barrier((half, give))
    arrived = swap_cores(give)
    other = swap_chips(pick(keep, 1 - chip) + pick(arrived, 1 - chip))
    inv, upper = factorise(half, swap_cores(half))
    return solve(inv, upper, keep, arrived, other)


def solution(mesh):
    return jax.shard_map(
        on_device,
        mesh=mesh,
        in_specs=(P("orb", ("prow", "pcol")), P("orb", ("prow", "pcol"))),
        out_specs=P(None, ("prow", "pcol", "orb")),
        check_vma=False,
    )
```

```python
import jax
import jax.numpy as jnp
from jax import lax
from jax.experimental import pallas as pl
from jax.experimental.pallas import tpu as pltpu
from jax.sharding import PartitionSpec as P

F32 = jnp.float32
HI = lax.Precision.HIGHEST
ROW0 = (((0,), (0,)), ((), ()))
NB = 128
PANEL = 512
FIRST_K = 2304
SECOND_K = 2816
CHUNK_K = 1024
HALVES = (((0, 0), (0, 1), (0, 2), (0, 3), (3, 3)), ((1, 1), (1, 2), (1, 3), (2, 2), (2, 3)))

CORE_SWAP = [(0, 1), (1, 0), (2, 3), (3, 2)]
CHIP_SWAP = [(0, 2), (2, 0), (1, 3), (3, 1)]


def x_shift(k):
    return [(h * 4 + x, h * 4 + (x + k) % 4) for h in range(2) for x in range(4)]


Y_SWAP = [(c, (c + 4) % 8) for c in range(8)]


def spread(v):
    return jnp.broadcast_to(v, (8, NB))


def reciprocal(v):
    return pl.reciprocal(v, approx=True)


def held_group(q):
    z, rest = divmod(q, 8)
    y, x = divmod(rest, 4)
    return z * 8 + x * 2 + y


def three_way(v):
    high = v.astype(jnp.bfloat16).astype(F32)
    v = v - high
    mid = v.astype(jnp.bfloat16).astype(F32)
    return high, mid, v - mid


def inverse_factor(rows):
    rows = list(rows)
    groups, near_by, out = len(rows), 3, []
    lane = lax.broadcasted_iota(jnp.int32, (8, NB), 1)
    sub = lax.broadcasted_iota(jnp.int32, (8, NB), 0)
    at = [sub == s for s in range(8)]
    true_lane = (lane // 64) * 64 + ((lane // 8) % 2) * 32 + ((lane // 16) % 4) * 8 + lane % 8

    def lanes(v, b):
        return [spread(v[:, b + t : b + t + 1]) for t in range(8)]

    def row(v, s):
        return spread(v[s : s + 1, :])

    diag = lanes(rows[0], 8 * held_group(0))
    for q in range(groups):
        b = 8 * held_group(q)
        a = {(s, t): row(diag[t], s) for t in range(8) for s in range(t, 8)}
        here = (lane >= b) & (lane < b + 8)
        w = jnp.where(here, jnp.where(lane - b == sub, 1.0, 0.0), rows[q])
        near = range(q + 1, min(q + 1 + near_by, groups))
        far = range(q + 1 + near_by, groups)
        if q + 1 < groups:
            diag = lanes(rows[q + 1], 8 * held_group(q + 1))
        below = {g: lanes(rows[g], b) for g in near}
        for g in range(q + 1, groups):
            rows[g] = jnp.where(here, 0.0, rows[g])
        pivots = jnp.ones((8, NB), F32)
        for t in range(8):
            d = a[t, t]
            if t < 7:
                square = a[t + 1, t] * a[t + 1, t]
            r = reciprocal(d)
            pivots = jnp.where(at[t], d, pivots)
            m = {s: a[s, t] * r for s in range(t + 1, 8)}
            for u in range(t + 1, 8):
                for s in range(u, 8):
                    step = square * r if s == t + 1 else m[s] * a[u, t]
                    a[s, u] = a[s, u] - step
            if q + 1 < groups:
                mg = below[q + 1][t] * r
                for u in range(8):
                    diag[u] = diag[u] - mg * row(below[q + 1][t], u)
            pivot_row = row(w, t)
            if t < 7:
                m_col = jnp.zeros((8, NB), F32)
                for s in range(t + 1, 8):
                    m_col = jnp.where(at[s], m[s], m_col)
                w = w - m_col * pivot_row
            for g in near:
                mg = below[g][t] * r
                for u in range(t + 1, 8):
                    below[g][u] = below[g][u] - mg * a[u, t]
                rows[g] = rows[g] - mg * pivot_row
        if len(far):
            ah, am, al = three_way(w * reciprocal(pivots))
            bh, bm, bl = three_way(w)
            product = lax.dot_general(
                jnp.concatenate([ah, ah, am, ah, am, al], 0).astype(jnp.bfloat16),
                jnp.concatenate([bh, bm, bh, bl, bm, bh], 0).astype(jnp.bfloat16),
                ROW0,
                preferred_element_type=F32,
            )
            for g in far:
                h = 8 * held_group(g)
                rows[g] = rows[g] - product[h : h + 8]
        root = lax.rsqrt(pivots)
        root = root * (1.5 - (0.5 * pivots * root) * root)
        out.append(jnp.where(true_lane <= sub + 8 * q, w * root, 0.0))
    return out


def factor_kernel(mine_ref, other_ref, inv_ref, upper_ref, pair_ref):
    core = lax.axis_index("orb") % 2

    def place(ref, half):
        for k, (i, j) in enumerate(HALVES[half]):
            gram = ref[k]
            pair_ref[i * NB : (i + 1) * NB, j * NB : (j + 1) * NB] = gram * gram

    @pl.when(core == 0)
    def _():
        place(mine_ref, 0)
        place(other_ref, 1)

    @pl.when(core == 1)
    def _():
        place(other_ref, 0)
        place(mine_ref, 1)

    def step(j, carry):
        o = pl.multiple_of(j * NB, NB)
        rows = [
            pair_ref[pl.ds(o + 8 * held_group(q), 8), pl.ds(o, NB)] for q in range(NB // 8)
        ]
        inv = jnp.concatenate(inverse_factor(rows), 0)
        inv_ref[j] = inv
        for k in range(PANEL // NB - 1):

            @pl.when(j == k)
            def _():
                rest = (k + 1) * NB
                upper = jnp.dot(
                    inv,
                    pair_ref[k * NB : rest, rest:],
                    precision=HI,
                    preferred_element_type=F32,
                )
                upper_ref[k, :, rest:] = upper
                for i in range(rest, PANEL, NB):
                    pair_ref[i : i + NB, i:] -= lax.dot_general(
                        upper[:, i - rest : i - rest + NB],
                        upper[:, i - rest :],
                        ROW0,
                        precision=HI,
                        preferred_element_type=F32,
                    )

        return carry

    lax.fori_loop(0, PANEL // NB, step, 0)


def solve_kernel(inv_ref, upper_ref, keep_ref, arrived_ref, other_ref, out_ref):
    solved = []
    for j in range(PANEL // NB):
        cut = slice(j * NB, (j + 1) * NB)
        gram = keep_ref[cut, :] + arrived_ref[cut, :] + other_ref[cut, :]
        rest = gram * gram
        for i in range(j):
            rest -= lax.dot_general(
                upper_ref[i, :, cut], solved[i], ROW0, precision=HI, preferred_element_type=F32
            )
        x = jnp.dot(inv_ref[j], rest, precision=HI, preferred_element_type=F32)
        solved.append(x)
        out_ref[cut, :] = x


def factorise(mine, other):
    blocks = PANEL // NB
    return pl.pallas_call(
        factor_kernel,
        out_shape=(
            jax.ShapeDtypeStruct((blocks, NB, NB), F32),
            jax.ShapeDtypeStruct((blocks - 1, NB, PANEL), F32),
        ),
        scratch_shapes=[pltpu.VMEM((PANEL, PANEL), F32)],
        compiler_params=pltpu.CompilerParams(vmem_limit_bytes=40 << 20),
        cost_estimate=pl.CostEstimate(flops=30_000_000_000, bytes_accessed=3 << 20, transcendentals=0),
        name="factor",
    )(mine, other)


def solve(inv, upper, keep, arrived, other):
    return pl.pallas_call(
        solve_kernel,
        out_shape=jax.ShapeDtypeStruct(other.shape, F32),
        compiler_params=pltpu.CompilerParams(vmem_limit_bytes=40 << 20),
        name="solve",
    )(inv, upper, keep, arrived, other)


def z_shift(k):
    return [(z, (z + k) % 8) for z in range(8)]


def along_z(k, v):
    return lax.ppermute(v, "prow", z_shift(k))


def along_x(k, v):
    return lax.ppermute(v, "pcol", x_shift(k))


def after(v, *others):
    return lax.optimization_barrier((v,) + others)[0]


def gather_panel(panel):
    own = panel.T
    far = lax.ppermute(own, "pcol", Y_SWAP)
    first = lax.axis_index("pcol") < 4
    pair = jnp.where(first, jnp.concatenate([own, far], 0), jnp.concatenate([far, own], 0))
    left = pair[:, :FIRST_K]
    right = jnp.pad(pair[:, FIRST_K:], ((0, 0), (0, FIRST_K + SECOND_K - panel.shape[0])))

    x_steps = (0, -1, 1, 2)
    plane = jnp.concatenate([left, along_x(1, left), along_x(-1, left), along_x(2, left)], 0)
    planes, plane_z = [plane], [0]
    column, column_z = [right], [0]

    def turn(pieces, steps, s, *ties):
        up, down = pieces[-2:] if s > 1 else pieces * 2
        pieces += [along_z(1, after(up, *ties)), along_z(-1, after(down, *ties))]
        steps += [-s, s]

    turn(column, column_z, 1)
    turn(planes, plane_z, 1)
    turn(column, column_z, 2)
    turn(column, column_z, 3, *planes[1:3])
    column_z.append(4)
    column.append(along_z(1, column[-2]))
    turn(planes, plane_z, 2)
    column = jnp.concatenate(column, 0)
    half = column.shape[0] // 2
    column = after(column, *planes[3:5])
    x_up, x_down = along_x(1, column), along_x(-1, column)
    turn(planes, plane_z, 3)
    x_far = (
        along_x(1, after(x_up[:half], *planes[5:7])),
        along_x(-1, after(x_down[half:], *planes[5:7])),
    )
    planes.append(along_z(1, planes[-2]))
    plane_z.append(4)

    plane_places = [
        (n, 16 * k, dz, dx) for n, dz in enumerate(plane_z) for k, dx in enumerate(x_steps)
    ]
    columns, column_places = [], []
    for piece, dx, units in (
        (column, 0, range(8)),
        (x_up, -1, range(8)),
        (x_down, 1, range(8)),
        (x_far[0], 2, range(4)),
        (x_far[1], 2, range(4, 8)),
    ):
        column_places += [(len(columns), 16 * k, column_z[m], dx) for k, m in enumerate(units)]
        columns.append(piece)
    return (planes, plane_places), (columns, column_places)


def chunks(depth):
    return [slice(k, min(k + CHUNK_K, depth)) for k in range(0, depth, CHUNK_K)]


def stream(places, piece_refs, panel_ref, sems, window=None):
    z = lax.axis_index("prow")
    x = lax.axis_index("pcol") % 4
    units = [
        (piece, row, pl.multiple_of(lax.rem(z + dz + 8, 8) * 64 + lax.rem(x + dx + 4, 4) * 16, 16))
        for piece, row, dz, dx in places
    ]
    parts = chunks(panel_ref.shape[1])

    def window_copy(c):
        orbitals_ref, start, window_ref, window_sems = window
        first = parts[c].start
        size = min(parts[c].stop, orbitals_ref.shape[0] - start) - first
        return pltpu.make_async_copy(
            orbitals_ref.at[pl.ds(start + first, size), :],
            window_ref.at[pl.ds(first, size), :],
            window_sems.at[c],
        )

    def start_chunk(c):
        for piece, row, to in units:
            pltpu.make_async_copy(
                piece_refs[piece].at[pl.ds(row, 16), parts[c]],
                panel_ref.at[pl.ds(to, 16), parts[c]],
                sems.at[c],
            ).start()
        if window is not None:
            window_copy(c).start()

    for c in range(min(2, len(parts))):
        start_chunk(c)
    for c, part in enumerate(parts):
        here = panel_ref.at[:, part]
        pltpu.make_async_copy(here, here, sems.at[c]).wait()
        if window is not None:
            window_copy(c).wait()
        if c + 2 < len(parts):
            start_chunk(c + 2)
        yield c, part


def add_rows(panel_ref, window_ref, part, total_ref, started):
    quarter = total_ref.shape[2]
    gram = jnp.dot(panel_ref[:, part], window_ref[part, :], preferred_element_type=F32)
    for n in range(4):
        value = gram[:, n * quarter : (n + 1) * quarter]
        total_ref[n] = total_ref[n] + value if started else value


def panel_strips(panel_ref, part, before):
    strips = []
    for s in range(2):
        strip = lax.dot_general(
            panel_ref[s * 256 : (s + 1) * 256, part],
            panel_ref[s * 256 :, part],
            (((1,), (1,)), ((), ())),
            preferred_element_type=F32,
        )
        strips.append(strip if before is None else before[s] + strip)
    return strips


def put_blocks(strips, out_ref, before_ref=None):
    for h, blocks in enumerate(HALVES):
        for k, (i, j) in enumerate(blocks):
            s = i // 2
            i, j = i - 2 * s, j - 2 * s
            value = strips[s][i * NB : (i + 1) * NB, j * NB : (j + 1) * NB]
            out_ref[h, k] = value if before_ref is None else before_ref[h, k] + value


def first_kernel(places, pieces, *refs):
    orbitals_ref, panel_out, rows_out = refs[pieces : pieces + 3]
    panel_ref, window_ref, total_ref, block_ref, sems, window_sems, out_sems = refs[pieces + 3 :]
    window = (orbitals_ref, 0, window_ref, window_sems)
    strips = None
    for c, part in stream(places, refs[:pieces], panel_ref, sems, window):
        add_rows(panel_ref, window_ref, part, total_ref, c > 0)
        if part.stop == FIRST_K:
            send_rows = pltpu.make_async_copy(total_ref, rows_out, out_sems.at[0])
            send_rows.start()
        strips = panel_strips(panel_ref, part, strips)
    put_blocks(strips, block_ref)
    send_panel = pltpu.make_async_copy(block_ref, panel_out, out_sems.at[1])
    send_panel.start()
    send_rows.wait()
    send_panel.wait()


def panel_kernel(places, pieces, *refs):
    before_ref, give_ref, keep_ref = refs[pieces : pieces + 3]
    panel_ref, total_ref, start_ref, sems, out_sems = refs[pieces + 3 :]
    core = lax.axis_index("orb") % 2
    strips = None
    for c, part in stream(places, refs[:pieces], panel_ref, sems):
        if c == 0:
            before = pltpu.make_async_copy(before_ref, start_ref, out_sems.at[2])
            before.start()
        strips = panel_strips(panel_ref, part, strips)
    before.wait()
    put_blocks(strips, total_ref, start_ref)
    sends = [
        pltpu.make_async_copy(total_ref.at[1 - core], give_ref, out_sems.at[0]),
        pltpu.make_async_copy(total_ref.at[core], keep_ref, out_sems.at[1]),
    ]
    for send in sends:
        send.start()
    for send in sends:
        send.wait()


def rows_kernel(places, pieces, *refs):
    orbitals_ref, before_ref, *out_refs = refs[pieces : pieces + 6]
    panel_ref, window_ref, total_ref, start_ref, sems, window_sems, out_sems = refs[pieces + 6 :]
    core = lax.axis_index("orb") % 2
    chip = lax.axis_index("orb") // 2
    quarter = total_ref.shape[2]
    rows = orbitals_ref.shape[0] - FIRST_K
    window_ref[rows:, :] = jnp.zeros((SECOND_K - rows, orbitals_ref.shape[1]), jnp.bfloat16)
    window = (orbitals_ref, FIRST_K, window_ref, window_sems)
    for c, part in stream(places, refs[:pieces], panel_ref, sems, window):
        if c == 0:
            before = pltpu.make_async_copy(before_ref, start_ref, out_sems.at[4])
            before.start()
        if part.stop < SECOND_K:
            add_rows(panel_ref, window_ref, part, total_ref, c > 0)
    before.wait()
    sends = []
    for n, ref in enumerate(out_refs):
        which = 2 * (1 - chip if n < 2 else chip) + (core if n % 2 else 1 - core)
        columns = pl.ds(pl.multiple_of(which * quarter, quarter), quarter)
        gram = jnp.dot(
            panel_ref[:, part], window_ref[part, columns], preferred_element_type=F32
        )
        total_ref[which] = total_ref[which] + (start_ref[which] + gram)
        sends.append(pltpu.make_async_copy(total_ref.at[which], ref, out_sems.at[n]))
        sends[-1].start()
    for send in sends:
        send.wait()


HBM = pl.BlockSpec(memory_space=pl.ANY)
DMA = pltpu.SemaphoreType.DMA
ROOMY = pltpu.CompilerParams(vmem_limit_bytes=60 << 20)


def first_grams(pieces, places, orbitals):
    columns, count = orbitals.shape[1], len(chunks(FIRST_K))
    blocks, totals = (2, 5, NB, NB), (4, PANEL, columns // 4)
    return pl.pallas_call(
        lambda *refs: first_kernel(places, len(pieces), *refs),
        in_specs=[HBM] * (len(pieces) + 1),
        out_specs=[HBM] * 2,
        out_shape=(jax.ShapeDtypeStruct(blocks, F32), jax.ShapeDtypeStruct(totals, F32)),
        scratch_shapes=[
            pltpu.VMEM((PANEL, FIRST_K), jnp.bfloat16),
            pltpu.VMEM((FIRST_K, columns), jnp.bfloat16),
            pltpu.VMEM(totals, F32),
            pltpu.VMEM(blocks, F32),
            DMA((count,)),
            DMA((count,)),
            DMA((2,)),
        ],
        compiler_params=ROOMY,
        cost_estimate=pl.CostEstimate(flops=5_000_000_000, bytes_accessed=12 << 20, transcendentals=0),
        name="first_grams",
    )(*pieces, orbitals)


def panel_gram(pieces, places, before):
    out = jax.ShapeDtypeStruct((5, NB, NB), F32)
    return pl.pallas_call(
        lambda *refs: panel_kernel(places, len(pieces), *refs),
        in_specs=[HBM] * (len(pieces) + 1),
        out_specs=[HBM] * 2,
        out_shape=(out, out),
        scratch_shapes=[
            pltpu.VMEM((PANEL, SECOND_K), jnp.bfloat16),
            pltpu.VMEM((2, 5, NB, NB), F32),
            pltpu.VMEM((2, 5, NB, NB), F32),
            DMA((len(chunks(SECOND_K)),)),
            DMA((3,)),
        ],
        compiler_params=ROOMY,
        cost_estimate=pl.CostEstimate(flops=1_500_000_000, bytes_accessed=4 << 20, transcendentals=0),
        name="panel_gram",
    )(*pieces, before)


def row_gram(pieces, places, orbitals, before):
    columns, count = orbitals.shape[1], len(chunks(SECOND_K))
    out = jax.ShapeDtypeStruct((PANEL, columns // 4), F32)
    return pl.pallas_call(
        lambda *refs: rows_kernel(places, len(pieces), *refs),
        in_specs=[HBM] * (len(pieces) + 2),
        out_specs=[HBM] * 4,
        out_shape=(out,) * 4,
        scratch_shapes=[
            pltpu.VMEM((PANEL, SECOND_K), jnp.bfloat16),
            pltpu.VMEM((SECOND_K, columns), jnp.bfloat16),
            pltpu.VMEM((4, PANEL, columns // 4), F32),
            pltpu.VMEM((4, PANEL, columns // 4), F32),
            DMA((count,)),
            DMA((count,)),
            DMA((5,)),
        ],
        compiler_params=ROOMY,
        cost_estimate=pl.CostEstimate(flops=4_000_000_000, bytes_accessed=12 << 20, transcendentals=0),
        name="row_gram",
    )(*pieces, orbitals, before)


def swap_cores(v):
    return lax.ppermute(v, "orb", CORE_SWAP)


def swap_chips(v):
    return lax.ppermute(v, "orb", CHIP_SWAP)


def on_device(panel_orbitals, orbitals):
    (first, first_places), (second, second_places) = gather_panel(panel_orbitals)
    panel, rows = first_grams(first, first_places, orbitals)
    give, keep = panel_gram(second, second_places, panel)
    half = keep + swap_cores(give)
    half, second = lax.optimization_barrier((half, second))
    sent = swap_chips(half)
    give, keep, our_give, our_keep = row_gram(second, second_places, orbitals, rows)
    half = after(half, our_keep) + sent
    other = swap_chips(keep + swap_cores(give))
    arrived = swap_cores(our_give)
    inv, upper = factorise(half, swap_cores(half))
    return solve(inv, upper, our_keep, arrived, other)


def solution(mesh):
    return jax.shard_map(
        on_device,
        mesh=mesh,
        in_specs=(P("orb", ("prow", "pcol")), P("orb", ("prow", "pcol"))),
        out_specs=P(None, ("prow", "pcol", "orb")),
        check_vma=False,
    )
```

```python
import jax
import jax.numpy as jnp
from jax import lax
from jax.experimental import pallas as pl
from jax.experimental.pallas import tpu as pltpu
from jax.sharding import PartitionSpec as P

F32 = jnp.float32
HI = lax.Precision.HIGHEST
ROW0 = (((0,), (0,)), ((), ()))
NB = 128
PANEL = 512
FIRST_K = 1920
SECOND_K = 3200
CHUNK_K = 1024
HALVES = (((0, 0), (0, 1), (0, 2), (0, 3), (3, 3)), ((1, 1), (1, 2), (1, 3), (2, 2), (2, 3)))

CORE_SWAP = [(0, 1), (1, 0), (2, 3), (3, 2)]
CHIP_SWAP = [(0, 2), (2, 0), (1, 3), (3, 1)]


def x_shift(k):
    return [(h * 4 + x, h * 4 + (x + k) % 4) for h in range(2) for x in range(4)]


Y_SWAP = [(c, (c + 4) % 8) for c in range(8)]


def spread(v):
    return jnp.broadcast_to(v, (8, NB))


def reciprocal(v):
    return pl.reciprocal(v, approx=True)


def held_group(q):
    z, rest = divmod(q, 8)
    y, x = divmod(rest, 4)
    return z * 8 + x * 2 + y


def three_way(v):
    high = v.astype(jnp.bfloat16).astype(F32)
    v = v - high
    mid = v.astype(jnp.bfloat16).astype(F32)
    return high, mid, v - mid


def inverse_factor(rows):
    rows = list(rows)
    groups, near_by, out = len(rows), 3, []
    lane = lax.broadcasted_iota(jnp.int32, (8, NB), 1)
    sub = lax.broadcasted_iota(jnp.int32, (8, NB), 0)
    at = [sub == s for s in range(8)]
    true_lane = (lane // 64) * 64 + ((lane // 8) % 2) * 32 + ((lane // 16) % 4) * 8 + lane % 8

    def lanes(v, b):
        return [spread(v[:, b + t : b + t + 1]) for t in range(8)]

    def row(v, s):
        return spread(v[s : s + 1, :])

    diag = lanes(rows[0], 8 * held_group(0))
    for q in range(groups):
        b = 8 * held_group(q)
        a = {(s, t): row(diag[t], s) for t in range(8) for s in range(t, 8)}
        here = (lane >= b) & (lane < b + 8)
        w = jnp.where(here, jnp.where(lane - b == sub, 1.0, 0.0), rows[q])
        near = range(q + 1, min(q + 1 + near_by, groups))
        far = range(q + 1 + near_by, groups)
        if q + 1 < groups:
            diag = lanes(rows[q + 1], 8 * held_group(q + 1))
        below = {g: lanes(rows[g], b) for g in near}
        for g in range(q + 1, groups):
            rows[g] = jnp.where(here, 0.0, rows[g])
        pivots = jnp.ones((8, NB), F32)
        for t in range(8):
            d = a[t, t]
            if t < 7:
                square = a[t + 1, t] * a[t + 1, t]
            r = reciprocal(d)
            pivots = jnp.where(at[t], d, pivots)
            m = {s: a[s, t] * r for s in range(t + 1, 8)}
            for u in range(t + 1, 8):
                for s in range(u, 8):
                    step = square * r if s == t + 1 else m[s] * a[u, t]
                    a[s, u] = a[s, u] - step
            if q + 1 < groups:
                mg = below[q + 1][t] * r
                for u in range(8):
                    diag[u] = diag[u] - mg * row(below[q + 1][t], u)
            pivot_row = row(w, t)
            if t < 7:
                m_col = jnp.zeros((8, NB), F32)
                for s in range(t + 1, 8):
                    m_col = jnp.where(at[s], m[s], m_col)
                w = w - m_col * pivot_row
            for g in near:
                mg = below[g][t] * r
                for u in range(t + 1, 8):
                    below[g][u] = below[g][u] - mg * a[u, t]
                rows[g] = rows[g] - mg * pivot_row
        if len(far):
            ah, am, al = three_way(w * reciprocal(pivots))
            bh, bm, bl = three_way(w)
            product = lax.dot_general(
                jnp.concatenate([ah, ah, am, ah, am, al], 0).astype(jnp.bfloat16),
                jnp.concatenate([bh, bm, bh, bl, bm, bh], 0).astype(jnp.bfloat16),
                ROW0,
                preferred_element_type=F32,
            )
            for g in far:
                h = 8 * held_group(g)
                rows[g] = rows[g] - product[h : h + 8]
        root = lax.rsqrt(pivots)
        root = root * (1.5 - (0.5 * pivots * root) * root)
        out.append(jnp.where(true_lane <= sub + 8 * q, w * root, 0.0))
    return out


def factor_kernel(mine_ref, other_ref, inv_ref, upper_ref, pair_ref):
    core = lax.axis_index("orb") % 2

    def place(ref, half):
        for k, (i, j) in enumerate(HALVES[half]):
            gram = ref[k]
            pair_ref[i * NB : (i + 1) * NB, j * NB : (j + 1) * NB] = gram * gram

    @pl.when(core == 0)
    def _():
        place(mine_ref, 0)
        place(other_ref, 1)

    @pl.when(core == 1)
    def _():
        place(other_ref, 0)
        place(mine_ref, 1)

    def step(j, carry):
        o = pl.multiple_of(j * NB, NB)
        rows = [
            pair_ref[pl.ds(o + 8 * held_group(q), 8), pl.ds(o, NB)] for q in range(NB // 8)
        ]
        inv = jnp.concatenate(inverse_factor(rows), 0)
        inv_ref[j] = inv
        for k in range(PANEL // NB - 1):

            @pl.when(j == k)
            def _():
                rest = (k + 1) * NB
                upper = jnp.dot(
                    inv,
                    pair_ref[k * NB : rest, rest:],
                    precision=HI,
                    preferred_element_type=F32,
                )
                upper_ref[k, :, rest:] = upper
                for i in range(rest, PANEL, NB):
                    pair_ref[i : i + NB, i:] -= lax.dot_general(
                        upper[:, i - rest : i - rest + NB],
                        upper[:, i - rest :],
                        ROW0,
                        precision=HI,
                        preferred_element_type=F32,
                    )

        return carry

    lax.fori_loop(0, PANEL // NB, step, 0)


def solve_kernel(inv_ref, upper_ref, keep_ref, arrived_ref, other_ref, out_ref):
    solved = []
    for j in range(PANEL // NB):
        cut = slice(j * NB, (j + 1) * NB)
        gram = keep_ref[cut, :] + arrived_ref[cut, :] + other_ref[cut, :]
        rest = gram * gram
        for i in range(j):
            rest -= lax.dot_general(
                upper_ref[i, :, cut], solved[i], ROW0, precision=HI, preferred_element_type=F32
            )
        x = jnp.dot(inv_ref[j], rest, precision=HI, preferred_element_type=F32)
        solved.append(x)
        out_ref[cut, :] = x


def factorise(mine, other):
    blocks = PANEL // NB
    return pl.pallas_call(
        factor_kernel,
        out_shape=(
            jax.ShapeDtypeStruct((blocks, NB, NB), F32),
            jax.ShapeDtypeStruct((blocks - 1, NB, PANEL), F32),
        ),
        scratch_shapes=[pltpu.VMEM((PANEL, PANEL), F32)],
        compiler_params=pltpu.CompilerParams(vmem_limit_bytes=40 << 20),
        cost_estimate=pl.CostEstimate(flops=30_000_000_000, bytes_accessed=3 << 20, transcendentals=0),
        name="factor",
    )(mine, other)


def solve(inv, upper, keep, arrived, other):
    return pl.pallas_call(
        solve_kernel,
        out_shape=jax.ShapeDtypeStruct(other.shape, F32),
        compiler_params=pltpu.CompilerParams(vmem_limit_bytes=40 << 20),
        name="solve",
    )(inv, upper, keep, arrived, other)


def z_shift(k):
    return [(z, (z + k) % 8) for z in range(8)]


def along_z(k, v):
    return lax.ppermute(v, "prow", z_shift(k))


def along_x(k, v):
    return lax.ppermute(v, "pcol", x_shift(k))


def after(v, *others):
    return lax.optimization_barrier((v,) + others)[0]


def gather_panel(panel):
    own = panel.T
    far = lax.ppermute(own, "pcol", Y_SWAP)
    first = lax.axis_index("pcol") < 4
    pair = jnp.where(first, jnp.concatenate([own, far], 0), jnp.concatenate([far, own], 0))
    left = pair[:, :FIRST_K]
    right = jnp.pad(pair[:, FIRST_K:], ((0, 0), (0, FIRST_K + SECOND_K - panel.shape[0])))

    x_steps = (0, -1, 1, 2)
    plane = jnp.concatenate([left, along_x(1, left), along_x(-1, left), along_x(2, left)], 0)
    planes, plane_z = [plane], [0]
    column, column_z = [right], [0]

    def turn(pieces, steps, s, *ties):
        up, down = pieces[-2:] if s > 1 else pieces * 2
        pieces += [along_z(1, after(up, *ties)), along_z(-1, after(down, *ties))]
        steps += [-s, s]

    turn(column, column_z, 1)
    turn(planes, plane_z, 1)
    turn(column, column_z, 2)
    batches = [jnp.concatenate(column, 0)]
    x_up, x_down = [along_x(1, batches[0])], [along_x(-1, batches[0])]
    turn(column, column_z, 3, *planes[1:3])
    column_z.append(4)
    column.append(along_z(1, column[-2]))
    turn(planes, plane_z, 2)
    batches.append(after(jnp.concatenate(column[5:], 0), *planes[3:5]))
    x_up.append(along_x(1, batches[1]))
    x_down.append(along_x(-1, batches[1]))
    x_far = [along_x(1, x_up[0][:48]), along_x(-1, x_down[0][48:])]
    turn(planes, plane_z, 3)
    x_far += [
        along_x(1, after(x_up[1][:16], *planes[5:7])),
        along_x(-1, after(x_down[1][16:], *planes[5:7])),
    ]
    planes.append(along_z(1, planes[-2]))
    plane_z.append(4)

    plane_places = [
        (n, 16 * k, dz, dx) for n, dz in enumerate(plane_z) for k, dx in enumerate(x_steps)
    ]
    columns, column_places = [], []
    for piece, dx, units in (
        (batches[0], 0, range(5)),
        (batches[1], 0, range(5, 8)),
        (x_up[0], -1, range(5)),
        (x_up[1], -1, range(5, 8)),
        (x_down[0], 1, range(5)),
        (x_down[1], 1, range(5, 8)),
        (x_far[0], 2, range(3)),
        (x_far[1], 2, range(3, 5)),
        (x_far[2], 2, range(5, 6)),
        (x_far[3], 2, range(6, 8)),
    ):
        column_places += [(len(columns), 16 * k, column_z[m], dx) for k, m in enumerate(units)]
        columns.append(piece)
    return (planes, plane_places), (columns, column_places)


def chunks(depth):
    return [slice(k, min(k + CHUNK_K, depth)) for k in range(0, depth, CHUNK_K)]


def stream(places, piece_refs, panel_ref, sems, window=None):
    z = lax.axis_index("prow")
    x = lax.axis_index("pcol") % 4
    units = [
        (piece, row, pl.multiple_of(lax.rem(z + dz + 8, 8) * 64 + lax.rem(x + dx + 4, 4) * 16, 16))
        for piece, row, dz, dx in places
    ]
    parts = chunks(panel_ref.shape[1])

    def window_copy(c):
        orbitals_ref, start, window_ref, window_sems = window
        first = parts[c].start
        size = min(parts[c].stop, orbitals_ref.shape[0] - start) - first
        return pltpu.make_async_copy(
            orbitals_ref.at[pl.ds(start + first, size), :],
            window_ref.at[pl.ds(first, size), :],
            window_sems.at[c],
        )

    def start_chunk(c):
        for piece, row, to in units:
            pltpu.make_async_copy(
                piece_refs[piece].at[pl.ds(row, 16), parts[c]],
                panel_ref.at[pl.ds(to, 16), parts[c]],
                sems.at[c],
            ).start()
        if window is not None:
            window_copy(c).start()

    for c in range(min(2, len(parts))):
        start_chunk(c)
    for c, part in enumerate(parts):
        here = panel_ref.at[:, part]
        pltpu.make_async_copy(here, here, sems.at[c]).wait()
        if window is not None:
            window_copy(c).wait()
        if c + 2 < len(parts):
            start_chunk(c + 2)
        yield c, part


def add_rows(panel_ref, window_ref, part, total_ref, started):
    quarter = total_ref.shape[2]
    gram = jnp.dot(panel_ref[:, part], window_ref[part, :], preferred_element_type=F32)
    for n in range(4):
        value = gram[:, n * quarter : (n + 1) * quarter]
        total_ref[n] = total_ref[n] + value if started else value


def panel_strips(panel_ref, part, before):
    strips = []
    for s in range(2):
        strip = lax.dot_general(
            panel_ref[s * 256 : (s + 1) * 256, part],
            panel_ref[s * 256 :, part],
            (((1,), (1,)), ((), ())),
            preferred_element_type=F32,
        )
        strips.append(strip if before is None else before[s] + strip)
    return strips


def put_blocks(strips, out_ref, before_ref=None):
    for h, blocks in enumerate(HALVES):
        for k, (i, j) in enumerate(blocks):
            s = i // 2
            i, j = i - 2 * s, j - 2 * s
            value = strips[s][i * NB : (i + 1) * NB, j * NB : (j + 1) * NB]
            out_ref[h, k] = value if before_ref is None else before_ref[h, k] + value


def first_kernel(places, pieces, *refs):
    orbitals_ref, panel_out, rows_out = refs[pieces : pieces + 3]
    panel_ref, window_ref, total_ref, block_ref, sems, window_sems, out_sems = refs[pieces + 3 :]
    window = (orbitals_ref, 0, window_ref, window_sems)
    strips = None
    for c, part in stream(places, refs[:pieces], panel_ref, sems, window):
        add_rows(panel_ref, window_ref, part, total_ref, c > 0)
        if part.stop == FIRST_K:
            send_rows = pltpu.make_async_copy(total_ref, rows_out, out_sems.at[0])
            send_rows.start()
        strips = panel_strips(panel_ref, part, strips)
    put_blocks(strips, block_ref)
    send_panel = pltpu.make_async_copy(block_ref, panel_out, out_sems.at[1])
    send_panel.start()
    send_rows.wait()
    send_panel.wait()


def panel_kernel(places, pieces, *refs):
    before_ref, give_ref, keep_ref = refs[pieces : pieces + 3]
    panel_ref, total_ref, start_ref, sems, out_sems = refs[pieces + 3 :]
    core = lax.axis_index("orb") % 2
    strips = None
    for c, part in stream(places, refs[:pieces], panel_ref, sems):
        if c == 0:
            before = pltpu.make_async_copy(before_ref, start_ref, out_sems.at[2])
            before.start()
        strips = panel_strips(panel_ref, part, strips)
    before.wait()
    put_blocks(strips, total_ref, start_ref)
    sends = [
        pltpu.make_async_copy(total_ref.at[1 - core], give_ref, out_sems.at[0]),
        pltpu.make_async_copy(total_ref.at[core], keep_ref, out_sems.at[1]),
    ]
    for send in sends:
        send.start()
    for send in sends:
        send.wait()


def rows_kernel(places, pieces, *refs):
    orbitals_ref, before_ref, *out_refs = refs[pieces : pieces + 6]
    panel_ref, window_ref, total_ref, start_ref, sems, window_sems, out_sems = refs[pieces + 6 :]
    core = lax.axis_index("orb") % 2
    chip = lax.axis_index("orb") // 2
    quarter = total_ref.shape[2]
    rows = orbitals_ref.shape[0] - FIRST_K
    window_ref[rows:, :] = jnp.zeros((SECOND_K - rows, orbitals_ref.shape[1]), jnp.bfloat16)
    window = (orbitals_ref, FIRST_K, window_ref, window_sems)
    for c, part in stream(places, refs[:pieces], panel_ref, sems, window):
        if c == 0:
            before = pltpu.make_async_copy(before_ref, start_ref, out_sems.at[4])
            before.start()
        if part.stop < SECOND_K:
            add_rows(panel_ref, window_ref, part, total_ref, c > 0)
    before.wait()
    sends = []
    for n, ref in enumerate(out_refs):
        which = 2 * (1 - chip if n < 2 else chip) + (core if n % 2 else 1 - core)
        columns = pl.ds(pl.multiple_of(which * quarter, quarter), quarter)
        gram = jnp.dot(
            panel_ref[:, part], window_ref[part, columns], preferred_element_type=F32
        )
        total_ref[which] = total_ref[which] + (start_ref[which] + gram)
        sends.append(pltpu.make_async_copy(total_ref.at[which], ref, out_sems.at[n]))
        sends[-1].start()
    for send in sends:
        send.wait()


HBM = pl.BlockSpec(memory_space=pl.ANY)
DMA = pltpu.SemaphoreType.DMA
ROOMY = pltpu.CompilerParams(vmem_limit_bytes=60 << 20)


def first_grams(pieces, places, orbitals):
    columns, count = orbitals.shape[1], len(chunks(FIRST_K))
    blocks, totals = (2, 5, NB, NB), (4, PANEL, columns // 4)
    return pl.pallas_call(
        lambda *refs: first_kernel(places, len(pieces), *refs),
        in_specs=[HBM] * (len(pieces) + 1),
        out_specs=[HBM] * 2,
        out_shape=(jax.ShapeDtypeStruct(blocks, F32), jax.ShapeDtypeStruct(totals, F32)),
        scratch_shapes=[
            pltpu.VMEM((PANEL, FIRST_K), jnp.bfloat16),
            pltpu.VMEM((FIRST_K, columns), jnp.bfloat16),
            pltpu.VMEM(totals, F32),
            pltpu.VMEM(blocks, F32),
            DMA((count,)),
            DMA((count,)),
            DMA((2,)),
        ],
        compiler_params=ROOMY,
        cost_estimate=pl.CostEstimate(flops=5_000_000_000, bytes_accessed=12 << 20, transcendentals=0),
        name="first_grams",
    )(*pieces, orbitals)


def panel_gram(pieces, places, before):
    out = jax.ShapeDtypeStruct((5, NB, NB), F32)
    return pl.pallas_call(
        lambda *refs: panel_kernel(places, len(pieces), *refs),
        in_specs=[HBM] * (len(pieces) + 1),
        out_specs=[HBM] * 2,
        out_shape=(out, out),
        scratch_shapes=[
            pltpu.VMEM((PANEL, SECOND_K), jnp.bfloat16),
            pltpu.VMEM((2, 5, NB, NB), F32),
            pltpu.VMEM((2, 5, NB, NB), F32),
            DMA((len(chunks(SECOND_K)),)),
            DMA((3,)),
        ],
        compiler_params=ROOMY,
        cost_estimate=pl.CostEstimate(flops=1_500_000_000, bytes_accessed=4 << 20, transcendentals=0),
        name="panel_gram",
    )(*pieces, before)


def row_gram(pieces, places, orbitals, before):
    columns, count = orbitals.shape[1], len(chunks(SECOND_K))
    out = jax.ShapeDtypeStruct((PANEL, columns // 4), F32)
    return pl.pallas_call(
        lambda *refs: rows_kernel(places, len(pieces), *refs),
        in_specs=[HBM] * (len(pieces) + 2),
        out_specs=[HBM] * 4,
        out_shape=(out,) * 4,
        scratch_shapes=[
            pltpu.VMEM((PANEL, SECOND_K), jnp.bfloat16),
            pltpu.VMEM((SECOND_K, columns), jnp.bfloat16),
            pltpu.VMEM((4, PANEL, columns // 4), F32),
            pltpu.VMEM((4, PANEL, columns // 4), F32),
            DMA((count,)),
            DMA((count,)),
            DMA((5,)),
        ],
        compiler_params=ROOMY,
        cost_estimate=pl.CostEstimate(flops=4_000_000_000, bytes_accessed=12 << 20, transcendentals=0),
        name="row_gram",
    )(*pieces, orbitals, before)


def swap_cores(v):
    return lax.ppermute(v, "orb", CORE_SWAP)


def swap_chips(v):
    return lax.ppermute(v, "orb", CHIP_SWAP)


def on_device(panel_orbitals, orbitals):
    (first, first_places), (second, second_places) = gather_panel(panel_orbitals)
    panel, rows = first_grams(first, first_places, orbitals)
    give, keep = panel_gram(second, second_places, panel)
    half = keep + swap_cores(give)
    half, second = lax.optimization_barrier((half, second))
    sent = swap_chips(half)
    give, keep, our_give, our_keep = row_gram(second, second_places, orbitals, rows)
    half = after(half, our_keep) + sent
    other = swap_chips(keep + swap_cores(give))
    arrived = swap_cores(our_give)
    inv, upper = factorise(half, swap_cores(half))
    return solve(inv, upper, our_keep, arrived, other)


def solution(mesh):
    return jax.shard_map(
        on_device,
        mesh=mesh,
        in_specs=(P("orb", ("prow", "pcol")), P("orb", ("prow", "pcol"))),
        out_specs=P(None, ("prow", "pcol", "orb")),
        check_vma=False,
    )
```
